32 devices in a mesh: fsdp: 8 (over y, x, core), replica: 4 (over z).
Axes of the slice: x: 2, y: 2, z: 4, core: 2. Of those that a mesh axis runs over, the one named last changes fastest.
Arguments:
- tokens: bfloat16 [4, 3072, 8192], P('replica', 'fsdp'), may hold values from -45 to 45
- key_grads: bfloat16 [4, 3072, 512], P('replica', 'fsdp'), may hold values from -45 to 45
- weights: float32 [4, 8192, 512], P('replica', 'fsdp'), may hold values from -6 to 6
- first_moment: float32 [4, 8192, 512], P('replica', 'fsdp'), may hold values from -4 to 4
- second_moment: float32 [4, 8192, 512], P('replica', 'fsdp'), may hold values from 0.01 to 1
- step_index: int32 [1], replicated, may hold values from 0 to 63
Outputs:
- new_weights: float32 [4, 8192, 512], P('replica', 'fsdp')
- new_first: float32 [4, 8192, 512], P('replica', 'fsdp')
- new_second: float32 [4, 8192, 512], P('replica', 'fsdp')
The draws below stay inside these ranges and needn't reach their ends.
All inputs are finite; a program needn't handle non-finite values.
Results may differ from the reference program's by a relative error of at most 0.0005.
Values may be sent and summed in bfloat16 or wider, within the bound.
A program may use at most 128 MiB of HBM per device.

```python
import math
import jax
import jax.numpy as jnp
from jax import lax

D = 8192
KVC = 512
REPLICAS = 4
TOKENS_R = 3072
LEVELS = 2


def draw_tokens(key, part):
    key_scale, key_base = jax.random.split(jax.random.fold_in(key, 11), 2)
    position = jnp.arange(D, dtype=jnp.float32) / D
    jitter = jax.random.uniform(key_scale, (D,), jnp.float32)
    column_scale = 10.0 ** (0.5 * position + 0.5 * jitter)
    values = jax.random.truncated_normal(key_base, -4.0, 4.0, (REPLICAS, TOKENS_R, D), jnp.float32)
    return (values * column_scale).astype(jnp.bfloat16)


def draw_key_grads(key, part):
    key_scale, key_base = jax.random.split(jax.random.fold_in(key, 23), 2)
    jitter = jax.random.uniform(key_scale, (KVC,), jnp.float32)
    column_scale = 10.0 ** jitter
    values = jax.random.truncated_normal(key_base, -4.0, 4.0, (REPLICAS, TOKENS_R, KVC), jnp.float32)
    return (values * column_scale).astype(jnp.bfloat16)


def level_of(key, extent, pieces, smallest, largest):
    def one(dim, parts):
        draws = jax.random.uniform(jax.random.fold_in(jax.random.fold_in(key, 6), dim), (parts,), jnp.float32, smallest / len(pieces), largest / len(pieces))
        return jnp.repeat(jnp.exp(draws), extent[dim] // parts).reshape((-1,) + (1,) * (len(extent) - dim - 1))

    factor_of = one(*pieces[0])
    for cut in pieces[1:]:
        factor_of = factor_of * one(*cut)
    return factor_of


def normal_values(key, shape, spread, bound, cuts=(), kind=jnp.bfloat16):
    result = spread * jax.random.normal(key, shape, jnp.float32)
    if cuts:
        result = result * level_of(key, shape, cuts, -0.22, 0.18)
    return jnp.clip(result, -bound, bound).astype(kind)


def setup_inputs(seed: int = 0) -> dict:
    streams_of = jax.random.split(jax.random.key(seed), 7)
    return {
        "tokens": draw_tokens(jax.random.fold_in(streams_of[6], 71), 0),
        "key_grads": draw_key_grads(jax.random.fold_in(streams_of[6], 71), 0),
        "weights": normal_values(streams_of[2], (REPLICAS, D, KVC), 1.0, 6.0, ((0, 4), (1, 8)), jnp.float32),
        "first_moment": normal_values(streams_of[3], (REPLICAS, D, KVC), 0.5, 4.0, ((0, 4), (1, 8)), jnp.float32),
        "second_moment": jnp.clip(jnp.exp(math.log(1.0) - 4.6051702 * jax.random.uniform(streams_of[4], (REPLICAS, D, KVC), jnp.float32) ** level_of(streams_of[4], (REPLICAS, D, KVC), ((0, 4), (1, 8)), -0.2, 0.2)), 0.01, 1.0),
        "step_index": jax.random.randint(streams_of[5], (1,), 0, 64).astype(jnp.int32),
    }


BETA_ONE = 0.9
BETA_TWO = 0.95
LEARN_RATE = 0.08
ADAM_EPS = 1e-08
NORM_EPS = 1e-06

def one_replica(operands):
    inputs, grads_out = operands
    return jnp.dot(inputs.T, grads_out, preferred_element_type=jnp.float32)

def reference(tokens, key_grads, weights, first_moment, second_moment, step_index):
    gradient = lax.map(one_replica, (tokens, key_grads))
    squares = lax.optimization_barrier(jnp.sum(gradient * gradient, axis=(1, 2), keepdims=True))
    grad_norm = jnp.sqrt(squares)
    clip_factor = jnp.minimum(1.0, math.sqrt(D * KVC) / (grad_norm + NORM_EPS))
    clipped = clip_factor * gradient
    new_first = BETA_ONE * first_moment + (1.0 - BETA_ONE) * clipped
    new_second = BETA_TWO * second_moment + (1.0 - BETA_TWO) * clipped * clipped
    step_count = (step_index[0] + 1).astype(jnp.float32)
    first_fix = 1.0 - jnp.power(BETA_ONE, step_count)
    second_fix = 1.0 - jnp.power(BETA_TWO, step_count)
    change = LEARN_RATE * (new_first / first_fix) / (jnp.sqrt(new_second / second_fix) + ADAM_EPS)
    updated = weights - change
    replica_ids = jnp.arange(REPLICAS, dtype=jnp.int32)
    distance = jnp.power(jnp.int32(2), (step_index[0] % LEVELS).astype(jnp.int32)).astype(jnp.int32)
    partner = jnp.where(replica_ids // distance % 2 == 0, replica_ids + distance, replica_ids - distance).astype(jnp.int32)
    new_weights = 0.5 * (updated + jnp.take(updated, partner, axis=0))
    return (new_weights, new_first, new_second)
```

```python
from functools import partial
import math

import jax
import jax.numpy as jnp
from jax import lax
from jax.experimental import pallas as pl
from jax.experimental.pallas import tpu as pltpu
from jax.sharding import PartitionSpec as P

BETA_ONE = 0.9
BETA_TWO = 0.95
LEARN_RATE = 0.08
ADAM_EPS = 1e-08
NORM_EPS = 1e-06
CODE_MAX = 32767.0
MESH = pl.DeviceIdType.MESH


def flip(index, mask):
    bit = 1
    while bit <= mask:
        if mask & bit:
            index = index + bit - 2 * bit * lax.rem(lax.div(index, bit), 2)
        bit *= 2
    return index


def send_plan(chips):
    bits = [1 << i for i in range(chips.bit_length() - 1)]
    orders = (bits, bits[::-1])
    plan = []
    for t in range(len(bits)):
        groups = []
        for s, order in enumerate(orders):
            later = order[t + 1:]
            masks = [sum(b for i, b in enumerate(later) if not pick >> (len(later) - 1 - i) & 1)
                     for pick in range(1 << len(later))]
            groups.append([(s, order[t], order[t] | mask) for mask in masks])
        for pair in zip(*groups):
            plan.extend(pair)
    return plan


def encode(x):
    top = jnp.max(jnp.abs(x), axis=0, keepdims=True)
    top = jnp.maximum(top, 1e-30)
    return code_with(x, CODE_MAX / top), top * (1.0 / CODE_MAX)


def code_with(x, inverse):
    return jnp.round(x * inverse).astype(jnp.int32).astype(jnp.int16)


def decode(codes, scale):
    return codes.astype(jnp.int32).astype(jnp.float32) * scale


def kernel(n, level, sizes, tokens, key_grads, weights, first, second, step,
           new_weights, new_first, new_second,
           tok, kgs, code_out, scale_out, code_in, scale_in, grad, wv, mv, vv,
           z_out, zs_out, z_in, zs_in, norms,
           in_sem, tok_sem, kg_sem, rs_sem, norm_sem, z_sem, out_sem):
    rows, half, tile, piece, sub = sizes
    depth = tokens.shape[1]
    cols = key_grads.shape[2]
    entries = tokens.shape[2] * cols
    plan = send_plan(n // 2)
    chunks = plan + [(0, 0, 0), (1, 0, 0)]
    sent = len(plan)
    me = lax.axis_index("fsdp")
    rep = lax.axis_index("replica")
    core = lax.rem(me, 2)
    twin = flip(me, 1)
    other = flip(rep, 1 << level)
    mine = pl.ds(pl.multiple_of(core * depth, 128), depth)

    def columns(mask, stream):
        return pl.ds(pl.multiple_of(flip(me, mask) * rows + stream * half, 128), half)

    kg_local = pltpu.make_async_copy(key_grads.at[0], kgs.at[mine], kg_sem.at[0])
    kg_local.start()
    tok_local = []
    for k, (s, _, delta) in enumerate(chunks):
        copy = pltpu.make_async_copy(
            tokens.at[0, :, columns(2 * delta, s)], tok.at[k, mine], tok_sem.at[0, k])
        copy.start()
        tok_local.append(copy)

    barrier = pltpu.get_barrier_semaphore()
    for mask in range(1, n):
        pl.semaphore_signal(barrier, inc=1, device_id={"fsdp": flip(me, mask)}, device_id_type=MESH)
    pl.semaphore_signal(barrier, inc=1, device_id={"replica": other}, device_id_type=MESH)
    pl.semaphore_wait(barrier, n)

    def remote(src, dst, send, recv, device):
        copy = pltpu.make_async_remote_copy(
            src_ref=src, dst_ref=dst, send_sem=send, recv_sem=recv,
            device_id=device, device_id_type=MESH)
        copy.start()
        return copy

    kg_far = remote(key_grads.at[0], kgs.at[mine], kg_sem.at[1], kg_sem.at[2], {"fsdp": twin})
    tok_far = []
    for k, (s, _, delta) in enumerate(chunks):
        tok_far.append(remote(
            tokens.at[0, :, columns(2 * delta + 1, s)], tok.at[k, mine],
            tok_sem.at[1, k], tok_sem.at[2, k], {"fsdp": twin}))

    state = []
    for i, (src, dst) in enumerate(((weights, wv), (first, mv), (second, vv))):
        copy = pltpu.make_async_copy(src.at[0], dst, in_sem.at[i])
        copy.start()
        state.append(copy)

    kg_local.wait()
    kg_far.wait_recv()

    def product(k, at):
        return lax.dot_general(
            tok[k, :, at], kgs[...], (((0,), (0,)), ((), ())),
            preferred_element_type=jnp.float32)

    def feeds(stream, delta):
        return [j for j, (s, b, d) in enumerate(plan) if s == stream and d ^ b == delta]

    passed = []
    for k, (s, bit, delta) in enumerate(plan):
        tok_local[k].wait()
        tok_far[k].wait_recv()
        sources = feeds(s, delta)
        for j in sources:
            passed[j][0].wait_recv()
            passed[j][1].wait_recv()

        def part(i, _, k=k, sources=sources):
            at = pl.ds(pl.multiple_of(i * tile, tile), tile)
            x = product(k, at)
            for j in sources:
                x = x + decode(code_in[j, at], scale_in[j, pl.ds(i, 1)])
            codes, scale = encode(x)
            code_out[k, at] = codes
            scale_out[k, pl.ds(i, 1)] = scale
            return 0

        lax.fori_loop(0, half // tile, part, 0)
        device = {"fsdp": flip(me, 2 * bit)}
        passed.append((
            remote(code_out.at[k], code_in.at[k], rs_sem.at[0, k], rs_sem.at[1, k], device),
            remote(scale_out.at[k], scale_in.at[k], rs_sem.at[2, k], rs_sem.at[3, k], device)))

    for s in range(2):
        k = sent + s
        tok_local[k].wait()
        tok_far[k].wait_recv()

        def own(i, _, k=k, s=s):
            at = pl.ds(pl.multiple_of(i * tile, tile), tile)
            grad[pl.ds(pl.multiple_of(s * half + i * tile, tile), tile)] = product(k, at)
            return 0

        lax.fori_loop(0, half // tile, own, 0)

    squares = jnp.zeros((8, cols), jnp.float32)
    ordered = [feeds(s, 0) for s in range(2)]
    for r in range(max(len(ordered[0]), 1)):
        for s in range(2):
            last = r + 1 >= len(ordered[s])
            source = ordered[s][r] if ordered[s] else None
            if source is not None:
                passed[source][0].wait_recv()
                passed[source][1].wait_recv()

            def add(i, total, source=source, s=s, last=last):
                at = pl.ds(pl.multiple_of(s * half + i * sub, sub), sub)
                x = grad[at]
                if source is not None:
                    scale = scale_in[source, pl.ds(lax.div(i * sub, tile), 1)]
                    x = x + decode(code_in[source, pl.ds(pl.multiple_of(i * sub, sub), sub)], scale)
                    grad[at] = x
                if last:
                    y = x * x
                    for g in range(sub // 8):
                        total = total + y[g * 8:(g + 1) * 8]
                return total

            squares = lax.fori_loop(0, half // sub, add, squares)

    flat = squares[:, :128]
    for g in range(1, cols // 128):
        flat = flat + squares[:, g * 128:(g + 1) * 128]
    norms[0] = flat
    told = []
    for mask in range(1, n):
        told.append(remote(norms.at[0], norms.at[mask], norm_sem.at[0, mask], norm_sem.at[1, mask],
                           {"fsdp": flip(me, mask)}))
    for copy in state:
        copy.wait()
    count = jnp.full((1, cols), step[0] + 1, jnp.int32).astype(jnp.float32)
    first_rate = LEARN_RATE / (1.0 - jnp.exp(count * math.log(BETA_ONE)))
    second_rate = 1.0 / (1.0 - jnp.exp(count * math.log(BETA_TWO)))
    total = norms[0]
    for mask in range(1, n):
        told[mask - 1].wait_recv()
        total = total + norms[mask]
    grad_norm = jnp.sqrt(jnp.sum(total, keepdims=True))
    clip = jnp.minimum(1.0, math.sqrt(entries) / (grad_norm + NORM_EPS))
    clip = jnp.broadcast_to(clip, (1, cols))

    swaps, outs = [], []
    for p in range(rows // piece):
        def adam(i, top, p=p):
            at = pl.ds(pl.multiple_of(p * piece + i * sub, sub), sub)
            clipped = clip * grad[at]
            f = BETA_ONE * mv[at] + (1.0 - BETA_ONE) * clipped
            v = BETA_TWO * vv[at] + (1.0 - BETA_TWO) * clipped * clipped
            mv[at] = f
            vv[at] = v
            u = wv[at] - first_rate * f / (jnp.sqrt(v * second_rate) + ADAM_EPS)
            wv[at] = u
            u = jnp.abs(u)
            for g in range(sub // 8):
                top = jnp.maximum(top, u[g * 8:(g + 1) * 8])
            return top

        top = lax.fori_loop(0, piece // sub, adam, jnp.full((8, cols), 1e-30, jnp.float32))
        top = jnp.max(top, axis=0, keepdims=True)
        zs_out[p] = jnp.broadcast_to(top * (1.0 / CODE_MAX), (8, cols))
        inverse = CODE_MAX / top

        def code(i, _, p=p, inverse=inverse):
            at = pl.ds(pl.multiple_of(p * piece + i * sub, sub), sub)
            z_out[at] = code_with(wv[at], inverse)
            return 0

        lax.fori_loop(0, piece // sub, code, 0)
        at = pl.ds(p * piece, piece)
        swaps.append((
            remote(z_out.at[at], z_in.at[at], z_sem.at[0, p], z_sem.at[1, p], {"replica": other}),
            remote(zs_out.at[p], zs_in.at[p], z_sem.at[2, p], z_sem.at[3, p], {"replica": other})))
        for i, (src, dst) in enumerate(((mv, new_first), (vv, new_second))):
            copy = pltpu.make_async_copy(src.at[at], dst.at[0, at], out_sem.at[i, p])
            copy.start()
            outs.append(copy)

    for p in range(rows // piece):
        swaps[p][0].wait_recv()
        swaps[p][1].wait_recv()

        def mean(i, _, p=p):
            at = pl.ds(pl.multiple_of(p * piece + i * sub, sub), sub)
            wv[at] = 0.5 * (wv[at] + decode(z_in[at], zs_in[p, 0:1]))
            return 0

        lax.fori_loop(0, piece // sub, mean, 0)
        at = pl.ds(p * piece, piece)
        copy = pltpu.make_async_copy(wv.at[at], new_weights.at[0, at], out_sem.at[2, p])
        copy.start()
        outs.append(copy)

    for copy in outs:
        copy.wait()
    for copy in [kg_far, *tok_far, *told]:
        copy.wait_send()
    for pair in passed + swaps:
        pair[0].wait_send()
        pair[1].wait_send()


def run_level(level, n, tokens, key_grads, weights, first, second, step):
    depth, width = tokens.shape[1:]
    cols = key_grads.shape[2]
    rows = weights.shape[1]
    half = rows // 2
    tile = min(256, half)
    piece = min(128, half)
    sub = min(32, piece)
    sent = max(n - 2, 1)
    pieces = rows // piece
    dma = pltpu.SemaphoreType.DMA
    hbm = pl.BlockSpec(memory_space=pl.ANY)
    out = jax.ShapeDtypeStruct(weights.shape, jnp.float32)
    block = pltpu.VMEM((rows, cols), jnp.float32)
    return pl.pallas_call(
        partial(kernel, n, level, (rows, half, tile, piece, sub)),
        out_shape=(out, out, out),
        in_specs=[hbm] * 5 + [pl.BlockSpec(memory_space=pltpu.SMEM)],
        out_specs=(hbm, hbm, hbm),
        scratch_shapes=[
            pltpu.VMEM((n, 2 * depth, half), jnp.bfloat16),
            pltpu.VMEM((2 * depth, cols), jnp.bfloat16),
            pltpu.VMEM((sent, half, cols), jnp.int16),
            pltpu.VMEM((sent, 8, cols), jnp.float32),
            pltpu.VMEM((sent, half, cols), jnp.int16),
            pltpu.VMEM((sent, 8, cols), jnp.float32),
            block, block, block, block,
            pltpu.VMEM((rows, cols), jnp.int16),
            pltpu.VMEM((pieces, 8, cols), jnp.float32),
            pltpu.VMEM((rows, cols), jnp.int16),
            pltpu.VMEM((pieces, 8, cols), jnp.float32),
            pltpu.VMEM((n, 8, 128), jnp.float32),
            dma((3,)), dma((3, n)), dma((3,)), dma((4, sent)), dma((2, n)), dma((4, pieces)), dma((3, pieces)),
        ],
        compiler_params=pltpu.CompilerParams(
            collective_id=level, has_side_effects=True, vmem_limit_bytes=48 * 1024 * 1024),
        cost_estimate=pl.CostEstimate(
            flops=2 * depth * width * cols, bytes_accessed=2 * depth * width + 24 * rows * cols,
            transcendentals=rows * cols),
        name=f"adam_swap_{level}",
    )(tokens, key_grads, weights, first, second, step)


def local(tokens, key_grads, weights, first_moment, second_moment, step_index):
    n = lax.axis_size("fsdp")
    levels = min(4, lax.axis_size("replica").bit_length() - 1)
    branches = [partial(run_level, level, n) for level in range(levels)]
    return lax.switch(step_index[0] % levels, branches,
                      tokens, key_grads, weights, first_moment, second_moment, step_index)


def solution(mesh):
    spec = P("replica", "fsdp", None)
    return jax.shard_map(local, mesh=mesh, in_specs=(spec,) * 5 + (P(),), out_specs=(spec,) * 3, check_vma=False)
```

```python
from functools import partial
import math

import jax
import jax.numpy as jnp
from jax import lax
from jax.experimental import pallas as pl
from jax.experimental.pallas import tpu as pltpu
from jax.sharding import PartitionSpec as P

BETA_ONE = 0.9
BETA_TWO = 0.95
LEARN_RATE = 0.08
ADAM_EPS = 1e-08
NORM_EPS = 1e-06
CODE_MAX = 32767.0
ROUNDS = 2
MESH = pl.DeviceIdType.MESH


def flip(index, mask):
    bit = 1
    while bit <= mask:
        if mask & bit:
            index = index + bit - 2 * bit * lax.rem(lax.div(index, bit), 2)
        bit *= 2
    return index


def send_plan(chips):
    bits = [1 << i for i in range(chips.bit_length() - 1)]
    orders = (bits, bits[::-1])
    steps = []
    for h in range(ROUNDS):
        for t in range(len(bits)):
            groups = []
            for s, order in enumerate(orders):
                later = order[t + 1:]
                masks = [sum(b for i, b in enumerate(later) if not pick >> (len(later) - 1 - i) & 1)
                         for pick in range(1 << len(later))]
                groups.append([(h, s, order[t], order[t] | mask) for mask in masks])
            steps.append([chunk for pair in zip(*groups) for chunk in pair])
    return steps


def row_pieces(rows, level):
    unit = rows // 16
    ahead = ((0, 2), (2, 2), (8, 2)) if level == 0 else ((0, 2), (8, 1))
    taken = {u for start, size in ahead for u in range(start, start + size)}
    after, start = [], 0
    while start < 16:
        if start in taken:
            start += 1
            continue
        size = 2 if start + 1 < 16 and start + 1 not in taken and start % 2 == 0 else 1
        after.append((start, size))
        start += size
    return [[(start * unit, size * unit) for start, size in part] for part in (ahead, after)]


def encode(x):
    top = jnp.max(jnp.abs(x), axis=0, keepdims=True)
    top = jnp.maximum(top, 1e-30)
    return code_with(x, CODE_MAX / top), top * (1.0 / CODE_MAX)


def code_with(x, inverse):
    return jnp.round(x * inverse).astype(jnp.int32).astype(jnp.int16)


def decode(codes, scale):
    return codes.astype(jnp.int32).astype(jnp.float32) * scale


def kernel(n, level, sub, tokens, key_grads, weights, first, second, step,
           new_weights, new_first, new_second,
           tok, kgs, code_out, scale_out, code_in, scale_in, grad, wv, mv, vv,
           z_out, zs_out, z_in, zs_in, e_out, es_out, e_in, es_in, norms, far_norm,
           in_sem, tok_sem, kg_sem, rs_sem, norm_sem, z_sem, e_sem, out_sem):
    depth = tokens.shape[1]
    cols = key_grads.shape[2]
    rows = weights.shape[1]
    half = rows // 2
    part = half // ROUNDS
    entries = tokens.shape[2] * cols
    steps = send_plan(n // 2)
    plan = [chunk for group in steps for chunk in group]
    owned = [(h, s, 0, 0) for h in range(ROUNDS) for s in range(2)]
    ahead, after = row_pieces(rows, level)
    me = lax.axis_index("fsdp")
    rep = lax.axis_index("replica")
    core = lax.rem(me, 2)
    twin = flip(me, 1)
    other = flip(rep, 1 << level)
    mine = pl.ds(pl.multiple_of(core * depth, 128), depth)
    chunks = plan + owned
    per = len(steps) // ROUNDS

    order = []
    for h in range(ROUNDS):
        sends = steps[h * per:(h + 1) * per]
        order += sends[:1]
        if h:
            order.append([c for c in owned if c[0] == h - 1])
        order += sends[1:]
    order.append([c for c in owned if c[0] == ROUNDS - 1])
    order = [chunks.index(c) for group in order for c in group]

    def columns(mask, h, s):
        return pl.ds(pl.multiple_of(flip(me, mask) * rows + s * half + h * part, 128), part)

    kg_local = pltpu.make_async_copy(key_grads.at[0], kgs.at[mine], kg_sem.at[0])
    kg_local.start()
    tok_local, tok_far = {}, {}
    for k in order:
        h, s, _, delta = chunks[k]
        tok_local[k] = pltpu.make_async_copy(
            tokens.at[0, :, columns(2 * delta, h, s)], tok.at[k, mine], tok_sem.at[0, k])
        tok_local[k].start()

    barrier = pltpu.get_barrier_semaphore()
    for mask in range(1, n):
        pl.semaphore_signal(barrier, inc=1, device_id={"fsdp": flip(me, mask)}, device_id_type=MESH)
    pl.semaphore_signal(barrier, inc=1, device_id={"replica": other}, device_id_type=MESH)
    pl.semaphore_wait(barrier, n)

    def remote(src, dst, send, recv, device):
        copy = pltpu.make_async_remote_copy(
            src_ref=src, dst_ref=dst, send_sem=send, recv_sem=recv,
            device_id=device, device_id_type=MESH)
        copy.start()
        return copy

    kg_far = remote(key_grads.at[0], kgs.at[mine], kg_sem.at[1], kg_sem.at[2], {"fsdp": twin})
    for k in order:
        h, s, _, delta = chunks[k]
        tok_far[k] = remote(
            tokens.at[0, :, columns(2 * delta + 1, h, s)], tok.at[k, mine],
            tok_sem.at[1, k], tok_sem.at[2, k], {"fsdp": twin})

    state = []
    for i, (src, dst) in enumerate(((weights, wv), (first, mv), (second, vv))):
        copy = pltpu.make_async_copy(src.at[0], dst, in_sem.at[i])
        copy.start()
        state.append(copy)

    kg_local.wait()
    kg_far.wait_recv()

    def product(k):
        tok_local[k].wait()
        tok_far[k].wait_recv()
        return lax.dot_general(
            tok[k], kgs[...], (((0,), (0,)), ((), ())), preferred_element_type=jnp.float32)

    def feeds(h, s, delta):
        return [j for j, c in enumerate(plan) if c[:2] == (h, s) and c[3] ^ c[2] == delta]

    def landed(j):
        passed[j][0].wait_recv()
        passed[j][1].wait_recv()

    def send(k):
        h, s, bit, delta = plan[k]
        sources = feeds(h, s, delta)
        for j in sources:
            landed(j)
        x = product(k)
        for j in sources:
            x = x + decode(code_in[j], scale_in[j, 0:1])
        codes, scale = encode(x)
        code_out[k] = codes
        scale_out[k] = jnp.broadcast_to(scale, (8, cols))
        device = {"fsdp": flip(me, 2 * bit)}
        passed[k] = (
            remote(code_out.at[k], code_in.at[k], rs_sem.at[0, k], rs_sem.at[1, k], device),
            remote(scale_out.at[k], scale_in.at[k], rs_sem.at[2, k], rs_sem.at[3, k], device))

    def own(h, squares):
        for s in range(2):
            grad[pl.ds(s * half + h * part, part)] = product(chunks.index((h, s, 0, 0)))
        sources = [feeds(h, s, 0) for s in range(2)]
        for r in range(max(len(sources[0]), 1)):
            for s in range(2):
                last = r + 1 >= len(sources[s])
                j = sources[s][r] if sources[s] else None
                if j is not None:
                    landed(j)

                def add(i, total, j=j, s=s, last=last):
                    at = pl.ds(pl.multiple_of(s * half + h * part + i * sub, sub), sub)
                    x = grad[at]
                    if j is not None:
                        x = x + decode(code_in[j, pl.ds(pl.multiple_of(i * sub, sub), sub)], scale_in[j, 0:1])
                        grad[at] = x
                    if last:
                        y = x * x
                        for g in range(sub // 8):
                            total = total + y[g * 8:(g + 1) * 8]
                    return total

                squares = lax.fori_loop(0, part // sub, add, squares)
        return squares

    def store(e, i, x):
        size = x.shape[0]
        e_out[e, i, pl.ds(0, size)], scale = encode(x)
        es_out[e, i] = jnp.broadcast_to(scale, (8, cols))

    def send_state(e):
        at = pl.ds(*ahead[e])
        size = pl.ds(0, ahead[e][1])
        store(e, 0, wv[at])
        store(e, 1, mv[at])
        store(e, 2, jnp.sqrt(vv[at]))
        early.append((
            remote(e_out.at[e, pl.ds(0, 3), size], e_in.at[e, pl.ds(0, 3), size],
                   e_sem.at[0, e], e_sem.at[1, e], {"replica": other}),
            remote(es_out.at[e, pl.ds(0, 3)], es_in.at[e, pl.ds(0, 3)],
                   e_sem.at[2, e], e_sem.at[3, e], {"replica": other})))

    def send_gradient(e):
        size = pl.ds(0, ahead[e][1])
        store(e, 3, grad[pl.ds(*ahead[e])])
        early.append((
            remote(e_out.at[e, 3, size], e_in.at[e, 3, size], e_sem.at[4, e], e_sem.at[5, e], {"replica": other}),
            remote(es_out.at[e, 3], es_in.at[e, 3], e_sem.at[6, e], e_sem.at[7, e], {"replica": other})))

    passed, early = {}, []
    squares = jnp.zeros((8, cols), jnp.float32)
    waiting = list(range(len(ahead)))
    count = 0
    for k in order:
        if k < len(plan):
            send(k)
            count += 1
            if count == 2:
                for copy in state:
                    copy.wait()
            if count >= 2 and count % 2 == 0 and waiting:
                send_state(waiting.pop(0))
            if count == 4:
                while waiting:
                    send_state(waiting.pop(0))
        elif chunks[k][1] == 0:
            h = chunks[k][0]
            squares = own(h, squares)
            if h == 0:
                for e in range(len(ahead)):
                    send_gradient(e)

    flat = squares[:, :128]
    for g in range(1, cols // 128):
        flat = flat + squares[:, g * 128:(g + 1) * 128]
    norms[0] = flat
    told = []
    for mask in range(1, n):
        told.append(remote(norms.at[0], norms.at[mask], norm_sem.at[0, mask], norm_sem.at[1, mask],
                           {"fsdp": flip(me, mask)}))
    taken = jnp.full((1, cols), step[0] + 1, jnp.int32).astype(jnp.float32)
    first_rate = LEARN_RATE / (1.0 - jnp.exp(taken * math.log(BETA_ONE)))
    second_rate = 1.0 / (1.0 - jnp.exp(taken * math.log(BETA_TWO)))

    def clip_of(total):
        grad_norm = jnp.sqrt(jnp.sum(total, keepdims=True))
        clip = jnp.minimum(1.0, math.sqrt(entries) / (grad_norm + NORM_EPS))
        return jnp.broadcast_to(clip, (1, cols))

    total = norms[0]
    for mask in range(1, n):
        told[mask - 1].wait_recv()
        total = total + norms[mask]
    far_norm[0] = total
    told_far = remote(far_norm.at[0], far_norm.at[1], norm_sem.at[0, 0], norm_sem.at[1, 0], {"replica": other})
    clip = clip_of(total)

    def adam(w, m, v, g, factor):
        clipped = factor * g
        f = BETA_ONE * m + (1.0 - BETA_ONE) * clipped
        v = BETA_TWO * v + (1.0 - BETA_TWO) * clipped * clipped
        return w - first_rate * f / (jnp.sqrt(v * second_rate) + ADAM_EPS), f, v

    def write(src, dst, at, sem):
        copy = pltpu.make_async_copy(src.at[at], dst.at[0, at], sem)
        copy.start()
        outs.append(copy)

    swaps, outs = [], []
    for p, (start, size) in enumerate(after):
        def update(i, top, start=start):
            at = pl.ds(pl.multiple_of(start + i * sub, sub), sub)
            u, mv[at], vv[at] = adam(wv[at], mv[at], vv[at], grad[at], clip)
            wv[at] = u
            u = jnp.abs(u)
            for g in range(sub // 8):
                top = jnp.maximum(top, u[g * 8:(g + 1) * 8])
            return top

        top = lax.fori_loop(0, size // sub, update, jnp.full((8, cols), 1e-30, jnp.float32))
        top = jnp.max(top, axis=0, keepdims=True)
        zs_out[p] = jnp.broadcast_to(top * (1.0 / CODE_MAX), (8, cols))
        inverse = CODE_MAX / top

        def code(i, _, start=start, inverse=inverse):
            at = pl.ds(pl.multiple_of(start + i * sub, sub), sub)
            z_out[at] = code_with(wv[at], inverse)
            return 0

        lax.fori_loop(0, size // sub, code, 0)
        at = pl.ds(start, size)
        swaps.append((
            remote(z_out.at[at], z_in.at[at], z_sem.at[0, p], z_sem.at[1, p], {"replica": other}),
            remote(zs_out.at[p], zs_in.at[p], z_sem.at[2, p], z_sem.at[3, p], {"replica": other})))
        write(mv, new_first, at, out_sem.at[0, p])
        write(vv, new_second, at, out_sem.at[1, p])

    told_far.wait_recv()
    far_clip = clip_of(far_norm[1])
    for pair in early:
        pair[0].wait_recv()
        pair[1].wait_recv()
    for e, (start, size) in enumerate(ahead):
        def both(i, _, e=e, start=start):
            at = pl.ds(pl.multiple_of(start + i * sub, sub), sub)
            here = pl.ds(pl.multiple_of(i * sub, sub), sub)
            w, m, root, g = [decode(e_in[e, j, here], es_in[e, j, 0:1]) for j in range(4)]
            far = adam(w, m, root * root, g, far_clip)[0]
            u, mv[at], vv[at] = adam(wv[at], mv[at], vv[at], grad[at], clip)
            wv[at] = 0.5 * (u + far)
            return 0

        lax.fori_loop(0, size // sub, both, 0)
        at = pl.ds(start, size)
        for i, (src, dst) in enumerate(((mv, new_first), (vv, new_second), (wv, new_weights))):
            write(src, dst, at, out_sem.at[i, len(after) + e])

    for p, (start, size) in enumerate(after):
        swaps[p][0].wait_recv()
        swaps[p][1].wait_recv()

        def mean(i, _, p=p, start=start):
            at = pl.ds(pl.multiple_of(start + i * sub, sub), sub)
            wv[at] = 0.5 * (wv[at] + decode(z_in[at], zs_in[p, 0:1]))
            return 0

        lax.fori_loop(0, size // sub, mean, 0)
        write(wv, new_weights, pl.ds(start, size), out_sem.at[2, p])

    for copy in outs:
        copy.wait()
    for copy in [kg_far, *tok_far.values(), *told, told_far]:
        copy.wait_send()
    for pair in [*passed.values(), *early, *swaps]:
        pair[0].wait_send()
        pair[1].wait_send()


def run_level(level, n, tokens, key_grads, weights, first, second, step):
    depth, width = tokens.shape[1:]
    cols = key_grads.shape[2]
    rows = weights.shape[1]
    part = rows // 2 // ROUNDS
    ahead, after = row_pieces(rows, level)
    tall = max(size for _, size in ahead)
    sub = min(32, min(size for _, size in ahead + after))
    count = ROUNDS * n
    sent = max(count - 2 * ROUNDS, 1)
    pieces = len(after)
    dma = pltpu.SemaphoreType.DMA
    hbm = pl.BlockSpec(memory_space=pl.ANY)
    out = jax.ShapeDtypeStruct(weights.shape, jnp.float32)
    block = pltpu.VMEM((rows, cols), jnp.float32)
    return pl.pallas_call(
        partial(kernel, n, level, sub),
        out_shape=(out, out, out),
        in_specs=[hbm] * 5 + [pl.BlockSpec(memory_space=pltpu.SMEM)],
        out_specs=(hbm, hbm, hbm),
        scratch_shapes=[
            pltpu.VMEM((count, 2 * depth, part), jnp.bfloat16),
            pltpu.VMEM((2 * depth, cols), jnp.bfloat16),
            pltpu.VMEM((sent, part, cols), jnp.int16),
            pltpu.VMEM((sent, 8, cols), jnp.float32),
            pltpu.VMEM((sent, part, cols), jnp.int16),
            pltpu.VMEM((sent, 8, cols), jnp.float32),
            block, block, block, block,
            pltpu.VMEM((rows, cols), jnp.int16),
            pltpu.VMEM((pieces, 8, cols), jnp.float32),
            pltpu.VMEM((rows, cols), jnp.int16),
            pltpu.VMEM((pieces, 8, cols), jnp.float32),
            pltpu.VMEM((len(ahead), 4, tall, cols), jnp.int16),
            pltpu.VMEM((len(ahead), 4, 8, cols), jnp.float32),
            pltpu.VMEM((len(ahead), 4, tall, cols), jnp.int16),
            pltpu.VMEM((len(ahead), 4, 8, cols), jnp.float32),
            pltpu.VMEM((n, 8, 128), jnp.float32),
            pltpu.VMEM((2, 8, 128), jnp.float32),
            dma((3,)), dma((3, count)), dma((3,)), dma((4, sent)), dma((2, n)), dma((4, pieces)),
            dma((8, len(ahead))), dma((3, pieces + len(ahead))),
        ],
        compiler_params=pltpu.CompilerParams(
            collective_id=level, has_side_effects=True, vmem_limit_bytes=48 * 1024 * 1024),
        cost_estimate=pl.CostEstimate(
            flops=2 * depth * width * cols, bytes_accessed=2 * depth * width + 24 * rows * cols,
            transcendentals=rows * cols),
        name=f"adam_swap_{level}",
    )(tokens, key_grads, weights, first, second, step)


def local(tokens, key_grads, weights, first_moment, second_moment, step_index):
    n = lax.axis_size("fsdp")
    levels = min(4, lax.axis_size("replica").bit_length() - 1)
    branches = [partial(run_level, level, n) for level in range(levels)]
    return lax.switch(step_index[0] % levels, branches,
                      tokens, key_grads, weights, first_moment, second_moment, step_index)


def solution(mesh):
    spec = P("replica", "fsdp", None)
    return jax.shard_map(local, mesh=mesh, in_specs=(spec,) * 5 + (P(),), out_specs=(spec,) * 3, check_vma=False)
```

```python
from functools import partial
import math

import jax
import jax.numpy as jnp
from jax import lax
from jax.experimental import pallas as pl
from jax.experimental.pallas import tpu as pltpu
from jax.sharding import PartitionSpec as P

BETA_ONE = 0.9
BETA_TWO = 0.95
LEARN_RATE = 0.08
ADAM_EPS = 1e-08
NORM_EPS = 1e-06
CODE_MAX = 32767.0
ROUNDS = 2
PARTS = 2
PLACE = pl.ANY
MESH = pl.DeviceIdType.MESH


def flip(index, mask):
    bit = 1
    while bit <= mask:
        if mask & bit:
            index = index + bit - 2 * bit * lax.rem(lax.div(index, bit), 2)
        bit *= 2
    return index


def send_plan(chips):
    bits = [1 << i for i in range(chips.bit_length() - 1)]
    orders = (bits, bits[::-1])
    steps = []
    for h in range(ROUNDS):
        for t in range(len(bits)):
            groups = []
            for s, order in enumerate(orders):
                later = order[t + 1:]
                masks = [sum(b for i, b in enumerate(later) if not pick >> (len(later) - 1 - i) & 1)
                         for pick in range(1 << len(later))]
                groups.append([(h, s, order[t], order[t] | mask) for mask in masks])
            steps.append([chunk for pair in zip(*groups) for chunk in pair])
    return steps


def row_pieces(rows, level):
    unit = rows // 16
    ahead = ((0, 2), (8, 2), (2, 2), (10, 2)) if level == 0 else ((0, 2), (8, 2))
    taken = {u for start, size in ahead for u in range(start, start + size)}
    after, start = [], 0
    while start < 16:
        if start in taken:
            start += 1
            continue
        size = 2 if start + 1 < 16 and start + 1 not in taken and start % 2 == 0 else 1
        after.append((start, size))
        start += size
    return [[(start * unit, size * unit) for start, size in part] for part in (ahead, after)]


def encode(x):
    top = jnp.max(jnp.abs(x), axis=0, keepdims=True)
    top = jnp.maximum(top, 1e-30)
    return code_with(x, CODE_MAX / top), top * (1.0 / CODE_MAX)


def code_with(x, inverse):
    return jnp.round(x * inverse).astype(jnp.int32).astype(jnp.int16)


def decode(codes, scale):
    return codes.astype(jnp.int32).astype(jnp.float32) * scale


def kernel(n, level, sub, tokens, key_grads, weights, first, second, step,
           new_weights, new_first, new_second,
           tok, kgs, code_out, scale_out, code_in, scale_in, grad, wv, mv, vv,
           z_out, zs_out, z_in, zs_in, e_out, es_out, e_in, es_in, norms, far_norm,
           in_sem, tok_sem, kg_sem, rs_sem, norm_sem, z_sem, e_sem, out_sem):
    depth = tokens.shape[1]
    cols = key_grads.shape[2]
    rows = weights.shape[1]
    half = rows // 2
    part = half // ROUNDS
    entries = tokens.shape[2] * cols
    steps = send_plan(n // 2)
    plan = [chunk for group in steps for chunk in group]
    owned = [(h, s, 0, 0) for h in range(ROUNDS) for s in range(2)]
    ahead, after = row_pieces(rows, level)
    me = lax.axis_index("fsdp")
    rep = lax.axis_index("replica")
    core = lax.rem(me, 2)
    twin = flip(me, 1)
    other = flip(rep, 1 << level)
    mine = pl.ds(pl.multiple_of(core * depth, 128), depth)
    chunks = plan + owned
    per = len(steps) // ROUNDS

    order = []
    for h in range(ROUNDS):
        sends = steps[h * per:(h + 1) * per]
        order += sends[:1]
        if h:
            order.append([c for c in owned if c[0] == h - 1])
        order += sends[1:]
    order.append([c for c in owned if c[0] == ROUNDS - 1])
    order = [chunks.index(c) for group in order for c in group]

    def columns(mask, h, s):
        return pl.ds(pl.multiple_of(flip(me, mask) * rows + s * half + h * part, 128), part)

    def load_state(e, i, src, dst):
        at = pl.ds(*(ahead + after)[e])
        copy = pltpu.make_async_copy(src.at[0, at], dst.at[at], in_sem.at[i, e])
        copy.start()
        return copy

    kg_local = pltpu.make_async_copy(key_grads.at[0], kgs.at[mine], kg_sem.at[0])
    kg_local.start()
    tok_local, tok_far = {}, {}
    for k in order:
        h, s, _, delta = chunks[k]
        tok_local[k] = pltpu.make_async_copy(
            tokens.at[0, :, columns(2 * delta, h, s)], tok.at[k, mine], tok_sem.at[0, k])
        tok_local[k].start()
    state = (weights, wv), (first, mv), (second, vv)
    loaded = [[load_state(e, i, *pair) for i, pair in enumerate(state)] for e in range(len(ahead))]

    barrier = pltpu.get_barrier_semaphore()
    for mask in range(1, n):
        pl.semaphore_signal(barrier, inc=1, device_id={"fsdp": flip(me, mask)}, device_id_type=MESH)
    pl.semaphore_signal(barrier, inc=1, device_id={"replica": other}, device_id_type=MESH)
    pl.semaphore_wait(barrier, n)

    def remote(src, dst, send, recv, device):
        copy = pltpu.make_async_remote_copy(
            src_ref=src, dst_ref=dst, send_sem=send, recv_sem=recv,
            device_id=device, device_id_type=MESH)
        copy.start()
        return copy

    kg_far = remote(key_grads.at[0], kgs.at[mine], kg_sem.at[1], kg_sem.at[2], {"fsdp": twin})
    queue = list(order)

    def fetch():
        if queue:
            k = queue.pop(0)
            h, s, _, delta = chunks[k]
            tok_far[k] = remote(
                tokens.at[0, :, columns(2 * delta + 1, h, s)], tok.at[k, mine],
                tok_sem.at[1, k], tok_sem.at[2, k], {"fsdp": twin})

    for _ in range(4):
        fetch()

    def product(k):
        tok_local[k].wait()
        tok_far[k].wait_recv()
        fetch()
        return lax.dot_general(
            tok[k], kgs[...], (((0,), (0,)), ((), ())), preferred_element_type=jnp.float32)

    def feeds(h, s, delta):
        return [j for j, c in enumerate(plan) if c[:2] == (h, s) and c[3] ^ c[2] == delta]

    def landed(j):
        passed[j][0].wait_recv()
        passed[j][1].wait_recv()

    def send(k):
        h, s, bit, delta = plan[k]
        sources = feeds(h, s, delta)
        for j in sources:
            landed(j)
        x = product(k)
        for j in sources:
            x = x + decode(code_in[j], scale_in[j, 0:1])
        codes, scale = encode(x)
        code_out[k] = codes
        scale_out[k] = jnp.broadcast_to(scale, (8, cols))
        device = {"fsdp": flip(me, 2 * bit)}
        passed[k] = (
            remote(code_out.at[k], code_in.at[k], rs_sem.at[0, k], rs_sem.at[1, k], device),
            remote(scale_out.at[k], scale_in.at[k], rs_sem.at[2, k], rs_sem.at[3, k], device))

    def own(h, squares):
        for s in range(2):
            grad[pl.ds(s * half + h * part, part)] = product(chunks.index((h, s, 0, 0)))
        sources = [feeds(h, s, 0) for s in range(2)]
        for r in range(max(len(sources[0]), 1)):
            for s in range(2):
                last = r + 1 >= len(sources[s])
                j = sources[s][r] if sources[s] else None
                if j is not None:
                    landed(j)

                def add(i, total, j=j, s=s, last=last):
                    at = pl.ds(pl.multiple_of(s * half + h * part + i * sub, sub), sub)
                    x = grad[at]
                    if j is not None:
                        x = x + decode(code_in[j, pl.ds(pl.multiple_of(i * sub, sub), sub)], scale_in[j, 0:1])
                        grad[at] = x
                    if last:
                        y = x * x
                        for g in range(sub // 8):
                            total = total + y[g * 8:(g + 1) * 8]
                    return total

                squares = lax.fori_loop(0, part // sub, add, squares)
        return squares

    def store(e, i, x):
        size = x.shape[0]
        e_out[e, i, pl.ds(0, size)], scale = encode(x)
        es_out[e, i] = jnp.broadcast_to(scale, (8, cols))

    def send_state(e):
        at = pl.ds(*ahead[e])
        size = pl.ds(0, ahead[e][1])
        for copy in loaded[e]:
            copy.wait()
        store(e, 0, wv[at])
        store(e, 1, mv[at])
        store(e, 2, jnp.sqrt(vv[at]))
        early.append((
            remote(e_out.at[e, pl.ds(0, 3), size], e_in.at[e, pl.ds(0, 3), size],
                   e_sem.at[0, e], e_sem.at[1, e], {"replica": other}),
            remote(es_out.at[e, pl.ds(0, 3)], es_in.at[e, pl.ds(0, 3)],
                   e_sem.at[2, e], e_sem.at[3, e], {"replica": other})))

    def send_gradient(e):
        size = pl.ds(0, ahead[e][1])
        store(e, 3, grad[pl.ds(*ahead[e])])
        early.append((
            remote(e_out.at[e, 3, size], e_in.at[e, 3, size], e_sem.at[4, e], e_sem.at[5, e], {"replica": other}),
            remote(es_out.at[e, 3], es_in.at[e, 3], e_sem.at[6, e], e_sem.at[7, e], {"replica": other})))

    passed, early = {}, []
    squares = jnp.zeros((8, cols), jnp.float32)
    send_state(0)
    send_state(1)
    kg_local.wait()
    kg_far.wait_recv()
    count = 0
    for k in order:
        if k < len(plan):
            send(k)
            count += 1
            if count == 2:
                for e in range(2, len(ahead)):
                    send_state(e)
                rest = [load_state(e, i, *pair) for e in range(len(ahead), len(ahead + after))
                        for i, pair in enumerate(state)]
        elif chunks[k][1] == 0:
            h = chunks[k][0]
            squares = own(h, squares)
            if h == 0:
                for e in range(len(ahead)):
                    send_gradient(e)

    flat = squares[:, :128]
    for g in range(1, cols // 128):
        flat = flat + squares[:, g * 128:(g + 1) * 128]
    norms[0] = flat
    told = []
    for mask in range(1, n):
        told.append(remote(norms.at[0], norms.at[mask], norm_sem.at[0, mask], norm_sem.at[1, mask],
                           {"fsdp": flip(me, mask)}))
    taken = jnp.full((1, cols), step[0] + 1, jnp.int32).astype(jnp.float32)
    first_rate = LEARN_RATE / (1.0 - jnp.exp(taken * math.log(BETA_ONE)))
    second_rate = 1.0 / (1.0 - jnp.exp(taken * math.log(BETA_TWO)))

    def clip_of(total):
        grad_norm = jnp.sqrt(jnp.sum(total, keepdims=True))
        clip = jnp.minimum(1.0, math.sqrt(entries) / (grad_norm + NORM_EPS))
        return jnp.broadcast_to(clip, (1, cols))

    total = norms[0]
    for mask in range(1, n):
        told[mask - 1].wait_recv()
        total = total + norms[mask]
    far_norm[0] = total
    told_far = remote(far_norm.at[0], far_norm.at[1], norm_sem.at[0, 0], norm_sem.at[1, 0], {"replica": other})
    clip = clip_of(total)

    def adam(w, m, v, g, factor):
        clipped = factor * g
        f = BETA_ONE * m + (1.0 - BETA_ONE) * clipped
        v = BETA_TWO * v + (1.0 - BETA_TWO) * clipped * clipped
        return w - first_rate * f / (jnp.sqrt(v * second_rate) + ADAM_EPS), f, v

    def write(src, dst, at, sem):
        copy = pltpu.make_async_copy(src.at[at], dst.at[0, at], sem)
        copy.start()
        outs.append(copy)

    for copy in rest:
        copy.wait()
    swaps, outs = [], []
    for p, (start, size) in enumerate(after):
        def update(i, top, start=start):
            at = pl.ds(pl.multiple_of(start + i * sub, sub), sub)
            u, mv[at], vv[at] = adam(wv[at], mv[at], vv[at], grad[at], clip)
            wv[at] = u
            u = jnp.abs(u)
            for g in range(sub // 8):
                top = jnp.maximum(top, u[g * 8:(g + 1) * 8])
            return top

        top = lax.fori_loop(0, size // sub, update, jnp.full((8, cols), 1e-30, jnp.float32))
        top = jnp.max(top, axis=0, keepdims=True)
        zs_out[p] = jnp.broadcast_to(top * (1.0 / CODE_MAX), (8, cols))
        inverse = CODE_MAX / top

        def code(i, _, start=start, inverse=inverse):
            at = pl.ds(pl.multiple_of(start + i * sub, sub), sub)
            z_out[at] = code_with(wv[at], inverse)
            return 0

        lax.fori_loop(0, size // sub, code, 0)
        at = pl.ds(start, size)
        swaps.append((
            remote(z_out.at[at], z_in.at[at], z_sem.at[0, p], z_sem.at[1, p], {"replica": other}),
            remote(zs_out.at[p], zs_in.at[p], z_sem.at[2, p], z_sem.at[3, p], {"replica": other})))
        write(mv, new_first, at, out_sem.at[0, p])
        write(vv, new_second, at, out_sem.at[1, p])

    told_far.wait_recv()
    far_clip = clip_of(far_norm[1])
    for pair in early:
        pair[0].wait_recv()
        pair[1].wait_recv()
    for e, (start, size) in enumerate(ahead):
        def both(i, _, e=e, start=start):
            at = pl.ds(pl.multiple_of(start + i * sub, sub), sub)
            here = pl.ds(pl.multiple_of(i * sub, sub), sub)
            w, m, root, g = [decode(e_in[e, j, here], es_in[e, j, 0:1]) for j in range(4)]
            far = adam(w, m, root * root, g, far_clip)[0]
            u, mv[at], vv[at] = adam(wv[at], mv[at], vv[at], grad[at], clip)
            wv[at] = 0.5 * (u + far)
            return 0

        lax.fori_loop(0, size // sub, both, 0)
        at = pl.ds(start, size)
        for i, (src, dst) in enumerate(((mv, new_first), (vv, new_second), (wv, new_weights))):
            write(src, dst, at, out_sem.at[i, len(after) + e])

    for p, (start, size) in enumerate(after):
        swaps[p][0].wait_recv()
        swaps[p][1].wait_recv()

        def mean(i, _, p=p, start=start):
            at = pl.ds(pl.multiple_of(start + i * sub, sub), sub)
            wv[at] = 0.5 * (wv[at] + decode(z_in[at], zs_in[p, 0:1]))
            return 0

        lax.fori_loop(0, size // sub, mean, 0)
        write(wv, new_weights, pl.ds(start, size), out_sem.at[2, p])

    for copy in outs:
        copy.wait()
    for copy in [kg_far, *tok_far.values(), *told, told_far]:
        copy.wait_send()
    for pair in [*passed.values(), *early, *swaps]:
        pair[0].wait_send()
        pair[1].wait_send()


def run_level(level, n, tokens, key_grads, weights, first, second, step):
    depth, width = tokens.shape[1:]
    cols = key_grads.shape[2]
    rows = weights.shape[1]
    part = rows // 2 // ROUNDS
    ahead, after = row_pieces(rows, level)
    tall = max(size for _, size in ahead)
    sub = min(32, min(size for _, size in ahead + after))
    count = ROUNDS * n
    sent = max(count - 2 * ROUNDS, 1)
    pieces = len(after)
    dma = pltpu.SemaphoreType.DMA
    hbm = pl.BlockSpec(memory_space=pl.ANY)
    out = jax.ShapeDtypeStruct(weights.shape, jnp.float32)
    block = pltpu.VMEM((rows, cols), jnp.float32)
    return pl.pallas_call(
        partial(kernel, n, level, sub),
        out_shape=(out, out, out),
        in_specs=[hbm] * 5 + [pl.BlockSpec(memory_space=pltpu.SMEM)],
        out_specs=(hbm, hbm, hbm),
        scratch_shapes=[
            pltpu.VMEM((count, 2 * depth, part), jnp.bfloat16),
            pltpu.VMEM((2 * depth, cols), jnp.bfloat16),
            pltpu.VMEM((sent, part, cols), jnp.int16),
            pltpu.VMEM((sent, 8, cols), jnp.float32),
            pltpu.VMEM((sent, part, cols), jnp.int16),
            pltpu.VMEM((sent, 8, cols), jnp.float32),
            block, block, block, block,
            pltpu.VMEM((rows, cols), jnp.int16),
            pltpu.VMEM((pieces, 8, cols), jnp.float32),
            pltpu.VMEM((rows, cols), jnp.int16),
            pltpu.VMEM((pieces, 8, cols), jnp.float32),
            pltpu.VMEM((len(ahead), 4, tall, cols), jnp.int16),
            pltpu.VMEM((len(ahead), 4, 8, cols), jnp.float32),
            pltpu.VMEM((len(ahead), 4, tall, cols), jnp.int16),
            pltpu.VMEM((len(ahead), 4, 8, cols), jnp.float32),
            pltpu.VMEM((n, 8, 128), jnp.float32),
            pltpu.VMEM((2, 8, 128), jnp.float32),
            dma((3, pieces + len(ahead))), dma((3, count)), dma((3,)), dma((4, sent)), dma((2, n)), dma((4, pieces)),
            dma((8, len(ahead))), dma((3, pieces + len(ahead))),
        ],
        compiler_params=pltpu.CompilerParams(
            collective_id=level, has_side_effects=True, vmem_limit_bytes=40 * 1024 * 1024),
        cost_estimate=pl.CostEstimate(
            flops=2 * depth * width * cols, bytes_accessed=2 * depth * width + 24 * rows * cols,
            transcendentals=rows * cols),
        name=f"adam_swap_{level}",
    )(tokens, key_grads, weights, first, second, step)


def move(*refs):
    sources, targets, sem = refs[:3], refs[3:6], refs[6]
    copies = []
    rows = sources[0].shape[1]
    for i, (src, dst) in enumerate(zip(sources, targets)):
        for j in range(PARTS):
            at = pl.ds(j * (rows // PARTS), rows // PARTS)
            copies.append(pltpu.make_async_copy(src.at[0, at], dst.at[0, at], sem.at[i, j]))
    for copy in copies:
        copy.start()
    for copy in copies:
        copy.wait()


def place(*results):
    out = jax.ShapeDtypeStruct(results[0].shape, jnp.float32)
    hbm = pl.BlockSpec(memory_space=pl.ANY)
    return pl.pallas_call(
        move, out_shape=(out,) * 3, in_specs=[pl.BlockSpec(memory_space=PLACE)] * 3, out_specs=(hbm,) * 3,
        scratch_shapes=[pltpu.SemaphoreType.DMA((3, PARTS))], name="place",
        compiler_params=pltpu.CompilerParams(vmem_limit_bytes=16 * 1024 * 1024),
    )(*results)


def local(tokens, key_grads, weights, first_moment, second_moment, step_index):
    n = lax.axis_size("fsdp")
    levels = min(4, lax.axis_size("replica").bit_length() - 1)
    branches = [partial(run_level, level, n) for level in range(levels)]
    return place(*lax.switch(step_index[0] % levels, branches,
                             tokens, key_grads, weights, first_moment, second_moment, step_index))


def solution(mesh):
    spec = P("replica", "fsdp", None)
    return jax.shard_map(local, mesh=mesh, in_specs=(spec,) * 5 + (P(),), out_specs=(spec,) * 3, check_vma=False)
```

```python
from functools import partial
import math

import jax
import jax.numpy as jnp
from jax import lax
from jax.experimental import pallas as pl
from jax.experimental.pallas import tpu as pltpu
from jax.sharding import PartitionSpec as P

BETA_ONE = 0.9
BETA_TWO = 0.95
LEARN_RATE = 0.08
ADAM_EPS = 1e-08
NORM_EPS = 1e-06
CODE_MAX = 32767.0
ROUNDS = 2
MESH = pl.DeviceIdType.MESH


def flip(index, mask):
    bit = 1
    while bit <= mask:
        if mask & bit:
            index = index + bit - 2 * bit * lax.rem(lax.div(index, bit), 2)
        bit *= 2
    return index


def send_plan(chips):
    bits = [1 << i for i in range(chips.bit_length() - 1)]
    orders = (bits, bits[::-1])
    steps = []
    for h in range(ROUNDS):
        for t in range(len(bits)):
            groups = []
            for s, order in enumerate(orders):
                later = order[t + 1:]
                masks = [sum(b for i, b in enumerate(later) if not pick >> (len(later) - 1 - i) & 1)
                         for pick in range(1 << len(later))]
                groups.append([(h, s, order[t], order[t] | mask) for mask in masks])
            steps.append([chunk for pair in zip(*groups) for chunk in pair])
    return steps


def row_pieces(rows, level):
    unit = rows // 16
    ahead = ((0, 2), (2, 2), (8, 2)) if level == 0 else ((0, 2), (8, 1))
    taken = {u for start, size in ahead for u in range(start, start + size)}
    after, start = [], 0
    while start < 16:
        if start in taken:
            start += 1
            continue
        size = 2 if start + 1 < 16 and start + 1 not in taken and start % 2 == 0 else 1
        after.append((start, size))
        start += size
    return [[(start * unit, size * unit) for start, size in part] for part in (ahead, after)]


def encode(x):
    top = jnp.max(jnp.abs(x), axis=0, keepdims=True)
    top = jnp.maximum(top, 1e-30)
    return code_with(x, CODE_MAX / top), top * (1.0 / CODE_MAX)


def code_with(x, inverse):
    return jnp.round(x * inverse).astype(jnp.int32).astype(jnp.int16)


def decode(codes, scale):
    return codes.astype(jnp.int32).astype(jnp.float32) * scale


def kernel(n, level, sub, tokens, key_grads, weights, first, second, step,
           new_weights, new_first, new_second,
           tok, kgs, code_out, scale_out, code_in, scale_in, grad, wv, mv, vv,
           z_out, zs_out, z_in, zs_in, e_out, es_out, e_in, es_in, norms, far_norm,
           in_sem, tok_sem, kg_sem, rs_sem, norm_sem, z_sem, e_sem, out_sem):
    depth = tokens.shape[1]
    cols = key_grads.shape[2]
    rows = weights.shape[1]
    half = rows // 2
    part = half // ROUNDS
    entries = tokens.shape[2] * cols
    steps = send_plan(n // 2)
    plan = [chunk for group in steps for chunk in group]
    owned = [(h, s, 0, 0) for h in range(ROUNDS) for s in range(2)]
    ahead, after = row_pieces(rows, level)
    me = lax.axis_index("fsdp")
    rep = lax.axis_index("replica")
    core = lax.rem(me, 2)
    twin = flip(me, 1)
    other = flip(rep, 1 << level)
    mine = pl.ds(pl.multiple_of(core * depth, 128), depth)
    chunks = plan + owned
    per = len(steps) // ROUNDS

    order = []
    for h in range(ROUNDS):
        sends = steps[h * per:(h + 1) * per]
        order += sends[:1]
        if h:
            order.append([c for c in owned if c[0] == h - 1])
        order += sends[1:]
    order.append([c for c in owned if c[0] == ROUNDS - 1])
    order = [chunks.index(c) for group in order for c in group]

    def columns(mask, h, s):
        return pl.ds(pl.multiple_of(flip(me, mask) * rows + s * half + h * part, 128), part)

    kg_local = pltpu.make_async_copy(key_grads.at[0], kgs.at[mine], kg_sem.at[0])
    kg_local.start()
    tok_local, tok_far = {}, {}
    for k in order:
        h, s, _, delta = chunks[k]
        tok_local[k] = pltpu.make_async_copy(
            tokens.at[0, :, columns(2 * delta, h, s)], tok.at[k, mine], tok_sem.at[0, k])
        tok_local[k].start()

    barrier = pltpu.get_barrier_semaphore()
    for mask in range(1, n):
        pl.semaphore_signal(barrier, inc=1, device_id={"fsdp": flip(me, mask)}, device_id_type=MESH)
    pl.semaphore_signal(barrier, inc=1, device_id={"replica": other}, device_id_type=MESH)
    pl.semaphore_wait(barrier, n)

    def remote(src, dst, send, recv, device):
        copy = pltpu.make_async_remote_copy(
            src_ref=src, dst_ref=dst, send_sem=send, recv_sem=recv,
            device_id=device, device_id_type=MESH)
        copy.start()
        return copy

    kg_far = remote(key_grads.at[0], kgs.at[mine], kg_sem.at[1], kg_sem.at[2], {"fsdp": twin})
    for k in order:
        h, s, _, delta = chunks[k]
        tok_far[k] = remote(
            tokens.at[0, :, columns(2 * delta + 1, h, s)], tok.at[k, mine],
            tok_sem.at[1, k], tok_sem.at[2, k], {"fsdp": twin})

    state = []
    for i, (src, dst) in enumerate(((weights, wv), (first, mv), (second, vv))):
        copy = pltpu.make_async_copy(src.at[0], dst, in_sem.at[i])
        copy.start()
        state.append(copy)

    kg_local.wait()
    kg_far.wait_recv()

    def product(k):
        tok_local[k].wait()
        tok_far[k].wait_recv()
        return lax.dot_general(
            tok[k], kgs[...], (((0,), (0,)), ((), ())), preferred_element_type=jnp.float32)

    def feeds(h, s, delta):
        return [j for j, c in enumerate(plan) if c[:2] == (h, s) and c[3] ^ c[2] == delta]

    def landed(j):
        passed[j][0].wait_recv()
        passed[j][1].wait_recv()

    def send(k):
        h, s, bit, delta = plan[k]
        sources = feeds(h, s, delta)
        for j in sources:
            landed(j)
        x = product(k)
        for j in sources:
            x = x + decode(code_in[j], scale_in[j, 0:1])
        codes, scale = encode(x)
        code_out[k] = codes
        scale_out[k] = jnp.broadcast_to(scale, (8, cols))
        device = {"fsdp": flip(me, 2 * bit)}
        passed[k] = (
            remote(code_out.at[k], code_in.at[k], rs_sem.at[0, k], rs_sem.at[1, k], device),
            remote(scale_out.at[k], scale_in.at[k], rs_sem.at[2, k], rs_sem.at[3, k], device))

    def own(h, squares):
        for s in range(2):
            grad[pl.ds(s * half + h * part, part)] = product(chunks.index((h, s, 0, 0)))
        sources = [feeds(h, s, 0) for s in range(2)]
        for r in range(max(len(sources[0]), 1)):
            for s in range(2):
                last = r + 1 >= len(sources[s])
                j = sources[s][r] if sources[s] else None
                if j is not None:
                    landed(j)

                def add(i, total, j=j, s=s, last=last):
                    at = pl.ds(pl.multiple_of(s * half + h * part + i * sub, sub), sub)
                    x = grad[at]
                    if j is not None:
                        x = x + decode(code_in[j, pl.ds(pl.multiple_of(i * sub, sub), sub)], scale_in[j, 0:1])
                        grad[at] = x
                    if last:
                        y = x * x
                        for g in range(sub // 8):
                            total = total + y[g * 8:(g + 1) * 8]
                    return total

                squares = lax.fori_loop(0, part // sub, add, squares)
        return squares

    def store(e, i, x):
        size = x.shape[0]
        e_out[e, i, pl.ds(0, size)], scale = encode(x)
        es_out[e, i] = jnp.broadcast_to(scale, (8, cols))

    def send_state(e):
        at = pl.ds(*ahead[e])
        size = pl.ds(0, ahead[e][1])
        store(e, 0, wv[at])
        store(e, 1, mv[at])
        store(e, 2, jnp.sqrt(vv[at]))
        early.append((
            remote(e_out.at[e, pl.ds(0, 3), size], e_in.at[e, pl.ds(0, 3), size],
                   e_sem.at[0, e], e_sem.at[1, e], {"replica": other}),
            remote(es_out.at[e, pl.ds(0, 3)], es_in.at[e, pl.ds(0, 3)],
                   e_sem.at[2, e], e_sem.at[3, e], {"replica": other})))

    def send_gradient(e):
        size = pl.ds(0, ahead[e][1])
        store(e, 3, grad[pl.ds(*ahead[e])])
        early.append((
            remote(e_out.at[e, 3, size], e_in.at[e, 3, size], e_sem.at[4, e], e_sem.at[5, e], {"replica": other}),
            remote(es_out.at[e, 3], es_in.at[e, 3], e_sem.at[6, e], e_sem.at[7, e], {"replica": other})))

    passed, early = {}, []
    squares = jnp.zeros((8, cols), jnp.float32)
    waiting = list(range(len(ahead)))
    count = 0
    for k in order:
        if k < len(plan):
            send(k)
            count += 1
            if count == 2:
                for copy in state:
                    copy.wait()
            if count >= 2 and count % 2 == 0 and waiting:
                send_state(waiting.pop(0))
            if count == 4:
                while waiting:
                    send_state(waiting.pop(0))
        elif chunks[k][1] == 0:
            h = chunks[k][0]
            squares = own(h, squares)
            if h == 0:
                for e in range(len(ahead)):
                    send_gradient(e)

    flat = squares[:, :128]
    for g in range(1, cols // 128):
        flat = flat + squares[:, g * 128:(g + 1) * 128]
    norms[0] = flat
    told = []
    for mask in range(1, n):
        told.append(remote(norms.at[0], norms.at[mask], norm_sem.at[0, mask], norm_sem.at[1, mask],
                           {"fsdp": flip(me, mask)}))
    taken = jnp.full((1, cols), step[0] + 1, jnp.int32).astype(jnp.float32)
    first_rate = LEARN_RATE / (1.0 - jnp.exp(taken * math.log(BETA_ONE)))
    second_rate = 1.0 / (1.0 - jnp.exp(taken * math.log(BETA_TWO)))

    def clip_of(total):
        grad_norm = jnp.sqrt(jnp.sum(total, keepdims=True))
        clip = jnp.minimum(1.0, math.sqrt(entries) / (grad_norm + NORM_EPS))
        return jnp.broadcast_to(clip, (1, cols))

    total = norms[0]
    for mask in range(1, n):
        told[mask - 1].wait_recv()
        total = total + norms[mask]
    far_norm[0] = total
    told_far = remote(far_norm.at[0], far_norm.at[1], norm_sem.at[0, 0], norm_sem.at[1, 0], {"replica": other})
    clip = clip_of(total)

    def adam(w, m, v, g, factor):
        clipped = factor * g
        f = BETA_ONE * m + (1.0 - BETA_ONE) * clipped
        v = BETA_TWO * v + (1.0 - BETA_TWO) * clipped * clipped
        return w - first_rate * f / (jnp.sqrt(v * second_rate) + ADAM_EPS), f, v

    def write(src, dst, at, sem):
        copy = pltpu.make_async_copy(src.at[at], dst.at[0, at], sem)
        copy.start()
        outs.append(copy)

    swaps, outs = [], []
    for p, (start, size) in enumerate(after):
        def update(i, top, start=start):
            at = pl.ds(pl.multiple_of(start + i * sub, sub), sub)
            u, mv[at], vv[at] = adam(wv[at], mv[at], vv[at], grad[at], clip)
            wv[at] = u
            u = jnp.abs(u)
            for g in range(sub // 8):
                top = jnp.maximum(top, u[g * 8:(g + 1) * 8])
            return top

        top = lax.fori_loop(0, size // sub, update, jnp.full((8, cols), 1e-30, jnp.float32))
        top = jnp.max(top, axis=0, keepdims=True)
        zs_out[p] = jnp.broadcast_to(top * (1.0 / CODE_MAX), (8, cols))
        inverse = CODE_MAX / top

        def code(i, _, start=start, inverse=inverse):
            at = pl.ds(pl.multiple_of(start + i * sub, sub), sub)
            z_out[at] = code_with(wv[at], inverse)
            return 0

        lax.fori_loop(0, size // sub, code, 0)
        at = pl.ds(start, size)
        swaps.append((
            remote(z_out.at[at], z_in.at[at], z_sem.at[0, p], z_sem.at[1, p], {"replica": other}),
            remote(zs_out.at[p], zs_in.at[p], z_sem.at[2, p], z_sem.at[3, p], {"replica": other})))
        write(mv, new_first, at, out_sem.at[0, p])
        write(vv, new_second, at, out_sem.at[1, p])

    told_far.wait_recv()
    far_clip = clip_of(far_norm[1])
    for pair in early:
        pair[0].wait_recv()
        pair[1].wait_recv()
    for e, (start, size) in enumerate(ahead):
        def both(i, _, e=e, start=start):
            at = pl.ds(pl.multiple_of(start + i * sub, sub), sub)
            here = pl.ds(pl.multiple_of(i * sub, sub), sub)
            w, m, root, g = [decode(e_in[e, j, here], es_in[e, j, 0:1]) for j in range(4)]
            far = adam(w, m, root * root, g, far_clip)[0]
            u, mv[at], vv[at] = adam(wv[at], mv[at], vv[at], grad[at], clip)
            wv[at] = 0.5 * (u + far)
            return 0

        lax.fori_loop(0, size // sub, both, 0)
        at = pl.ds(start, size)
        for i, (src, dst) in enumerate(((mv, new_first), (vv, new_second), (wv, new_weights))):
            write(src, dst, at, out_sem.at[i, len(after) + e])

    for p, (start, size) in enumerate(after):
        swaps[p][0].wait_recv()
        swaps[p][1].wait_recv()

        def mean(i, _, p=p, start=start):
            at = pl.ds(pl.multiple_of(start + i * sub, sub), sub)
            wv[at] = 0.5 * (wv[at] + decode(z_in[at], zs_in[p, 0:1]))
            return 0

        lax.fori_loop(0, size // sub, mean, 0)
        write(wv, new_weights, pl.ds(start, size), out_sem.at[2, p])

    for copy in outs:
        copy.wait()
    for copy in [kg_far, *tok_far.values(), *told, told_far]:
        copy.wait_send()
    for pair in [*passed.values(), *early, *swaps]:
        pair[0].wait_send()
        pair[1].wait_send()


def run_level(level, n, tokens, key_grads, weights, first, second, step):
    depth, width = tokens.shape[1:]
    cols = key_grads.shape[2]
    rows = weights.shape[1]
    part = rows // 2 // ROUNDS
    ahead, after = row_pieces(rows, level)
    tall = max(size for _, size in ahead)
    sub = min(32, min(size for _, size in ahead + after))
    count = ROUNDS * n
    sent = max(count - 2 * ROUNDS, 1)
    pieces = len(after)
    dma = pltpu.SemaphoreType.DMA
    hbm = pl.BlockSpec(memory_space=pl.ANY)
    out = jax.ShapeDtypeStruct(weights.shape, jnp.float32)
    block = pltpu.VMEM((rows, cols), jnp.float32)
    return pl.pallas_call(
        partial(kernel, n, level, sub),
        out_shape=(out, out, out),
        in_specs=[hbm] * 5 + [pl.BlockSpec(memory_space=pltpu.SMEM)],
        out_specs=(hbm, hbm, hbm),
        scratch_shapes=[
            pltpu.VMEM((count, 2 * depth, part), jnp.bfloat16),
            pltpu.VMEM((2 * depth, cols), jnp.bfloat16),
            pltpu.VMEM((sent, part, cols), jnp.int16),
            pltpu.VMEM((sent, 8, cols), jnp.float32),
            pltpu.VMEM((sent, part, cols), jnp.int16),
            pltpu.VMEM((sent, 8, cols), jnp.float32),
            block, block, block, block,
            pltpu.VMEM((rows, cols), jnp.int16),
            pltpu.VMEM((pieces, 8, cols), jnp.float32),
            pltpu.VMEM((rows, cols), jnp.int16),
            pltpu.VMEM((pieces, 8, cols), jnp.float32),
            pltpu.VMEM((len(ahead), 4, tall, cols), jnp.int16),
            pltpu.VMEM((len(ahead), 4, 8, cols), jnp.float32),
            pltpu.VMEM((len(ahead), 4, tall, cols), jnp.int16),
            pltpu.VMEM((len(ahead), 4, 8, cols), jnp.float32),
            pltpu.VMEM((n, 8, 128), jnp.float32),
            pltpu.VMEM((2, 8, 128), jnp.float32),
            dma((3,)), dma((3, count)), dma((3,)), dma((4, sent)), dma((2, n)), dma((4, pieces)),
            dma((8, len(ahead))), dma((3, pieces + len(ahead))),
        ],
        compiler_params=pltpu.CompilerParams(
            collective_id=level, has_side_effects=True, vmem_limit_bytes=48 * 1024 * 1024),
        cost_estimate=pl.CostEstimate(
            flops=2 * depth * width * cols, bytes_accessed=2 * depth * width + 24 * rows * cols,
            transcendentals=rows * cols),
        name=f"adam_swap_{level}",
    )(tokens, key_grads, weights, first, second, step)


def move(a, b, c, x, y, z):
    x[...] = a[...]
    y[...] = b[...]
    z[...] = c[...]


def place(*results):
    _, rows, cols = results[0].shape
    out = jax.ShapeDtypeStruct(results[0].shape, jnp.float32)
    block = pl.BlockSpec((1, rows // 4, cols), lambda i: (0, i, 0))
    return pl.pallas_call(
        move, grid=(4,), out_shape=(out,) * 3, in_specs=[block] * 3, out_specs=(block,) * 3, name="place",
        compiler_params=pltpu.CompilerParams(vmem_limit_bytes=16 * 1024 * 1024),
    )(*results)


def local(tokens, key_grads, weights, first_moment, second_moment, step_index):
    n = lax.axis_size("fsdp")
    levels = min(4, lax.axis_size("replica").bit_length() - 1)
    branches = [partial(run_level, level, n) for level in range(levels)]
    return place(*lax.switch(step_index[0] % levels, branches,
                             tokens, key_grads, weights, first_moment, second_moment, step_index))


def solution(mesh):
    spec = P("replica", "fsdp", None)
    return jax.shard_map(local, mesh=mesh, in_specs=(spec,) * 5 + (P(),), out_specs=(spec,) * 3, check_vma=False)
```
